128 devices in a mesh: dp: 32 (over z, x, core), group: 4 (over y).
Axes of the slice: x: 4, y: 4, z: 4, core: 2. Of those that a mesh axis runs over, the one named last changes fastest.
Arguments:
- queries: bfloat16 [20480, 1024], P(('dp', 'group')), may hold values from -120 to 120
- passages: bfloat16 [20480, 1024], P(('dp', 'group')), may hold values from -12 to 12
- weight: bfloat16 [1024, 1024], P(('dp', 'group')), may hold values from -0.1875 to 0.1875
- block_list: int32 [128, 32], replicated, may hold values from 0 to 31, as said below
- list_len: int32 [128], replicated, may hold values from 2 to 32, as said below
Outputs:
- losses: float32 [20480], P(('dp', 'group'))
- grad_queries: bfloat16 [20480, 1024], P(('dp', 'group'))
- grad_passages: bfloat16 [20480, 1024], P(('dp', 'group'))
- grad_weight: float32 [1024, 1024], P(('dp', 'group'))
The draws below stay inside these ranges and needn't reach their ends.
Inputs may be any that keep to these rules, and one draw needn't show every extreme that they name: `block_list`: each row is an order of 0 to 31 whose first entry is the device's own dp index d. `list_len`: some device scores all 32 blocks of its domain and some only 2.
All inputs are finite; a program needn't handle non-finite values.
Results may differ from the reference program's by a relative error of at most 0.011.
Values may be sent and summed in bfloat16 or wider, within the bound.
No kernel may reach another device: no remote copies, remote signals or barrier semaphores. Data moves between devices by JAX's collectives and lax.ppermute only.
A program may use at most 128 MiB of HBM per device.

```python
import jax
import jax.numpy as jnp
from jax import lax

D = 1024
R = 160
TOKENS = 20480
N_DP = 32
N_GROUP = 4


def shared_passages(key, spread, tied):
    base = jax.random.normal(jax.random.fold_in(key, 101), (TOKENS, D), jnp.float32)
    factor = jnp.exp(jax.random.uniform(jax.random.fold_in(key, 102), (TOKENS, 1), jnp.float32, -spread, spread))
    values = base * factor
    row_ids = jnp.arange(TOKENS) % R
    partner = jnp.roll(values, 2, axis=0)
    chosen = (row_ids >= 2) & (row_ids < 4)
    values = jnp.where(chosen[:, None] & (tied > 0.0), partner, values)
    return jnp.clip(values, -12.0, 12.0)


def draw_passages(key, part):
    values = shared_passages(key, 0.0, 0.0)
    return values.astype(jnp.bfloat16)


def draw_queries(key, part):
    own_key = jax.random.fold_in(key, 5)
    values = jax.random.normal(own_key, (TOKENS, D), jnp.float32)
    return jnp.clip(values, -120.0, 120.0).astype(jnp.bfloat16)


def draw_block_list(key, part):
    key = jax.random.fold_in(key, 7)
    device_keys = jax.random.split(key, N_DP * N_GROUP)
    orders = jax.vmap(lambda one_key: jax.random.permutation(one_key, N_DP))(device_keys).astype(jnp.int32)
    owners = (jnp.arange(N_DP * N_GROUP, dtype=jnp.int32) // N_GROUP).astype(jnp.int32)
    leading = orders[:, :1]
    swapped = jnp.where(orders == owners[:, None], leading, orders)
    return swapped.at[:, 0].set(owners)


def draw_list_len(key, part):
    key = jax.random.fold_in(key, 9)
    count = N_DP * N_GROUP
    lengths = jax.random.randint(key, (count,), 2, N_DP + 1).astype(jnp.int32)
    first = jax.random.randint(jax.random.fold_in(key, 1), (), 0, count)
    second = (first + 1 + jax.random.randint(jax.random.fold_in(key, 2), (), 0, count - 1)) % count
    device_ids = jnp.arange(count)
    lengths = jnp.where(device_ids == first, N_DP, lengths)
    lengths = jnp.where(device_ids == second, 2, lengths)
    return lengths.astype(jnp.int32)


def levels(rng, shape, pieces, least, high):
    factor_of, own = 1.0, jax.random.fold_in(rng, 6)
    for axis_at, blocks in pieces:
        heights = jnp.exp(jax.random.uniform(jax.random.fold_in(own, axis_at), (blocks,), jnp.float32, least / len(pieces), high / len(pieces)))
        factor_of = factor_of * jnp.repeat(heights, shape[axis_at] // blocks).reshape([-1 if axis == axis_at else 1 for axis in range(len(shape))])
    return factor_of


def centred(rng, extent, width, limit, cuts=(), kind=jnp.bfloat16):
    loudness = levels(rng, extent, cuts, -0.22, 0.18) if cuts else 1.0
    drawn = jax.random.normal(rng, extent, jnp.float32) * width * loudness
    return jnp.minimum(jnp.maximum(drawn, -limit), limit).astype(kind)


def setup_inputs(seed: int = 0) -> dict:
    keys = jax.random.split(jax.random.key(seed), 6)
    queries = draw_queries(jax.random.fold_in(keys[5], 71), 0)
    passages = draw_passages(jax.random.fold_in(keys[5], 71), 0)
    weight = centred(keys[2], (D, D), D ** -0.5, 0.1875, ((0, 128),))
    block_list = draw_block_list(jax.random.fold_in(keys[5], 71), 0)
    list_len = draw_list_len(jax.random.fold_in(keys[5], 71), 0)
    return {"queries": queries, "passages": passages, "weight": weight, "block_list": block_list, "list_len": list_len}


def score_rows(query_emb, domain, listed_row, owner, row_count, logit_scale):
    column_count = domain.shape[0]
    scores = logit_scale * jnp.dot(query_emb, domain.T, preferred_element_type=jnp.float32)
    col_live = jnp.repeat(listed_row, row_count)
    masked = jnp.where(col_live[None, :], scores, -1e30)
    row_max = jnp.max(masked, axis=1)
    log_total = row_max + jnp.log(jnp.sum(jnp.exp(masked - row_max[:, None]), axis=1))
    probs = jnp.where(col_live[None, :], jnp.exp(scores - log_total[:, None]), 0.0)
    column_ids = jnp.arange(column_count, dtype=jnp.int32)
    target = owner * row_count + jnp.arange(row_count, dtype=jnp.int32)
    positive = column_ids[None, :] == target[:, None]
    pos_score = jnp.sum(jnp.where(positive, scores, 0.0), axis=1)
    grads = (probs - positive.astype(jnp.float32)).astype(jnp.bfloat16)
    return log_total - pos_score, grads


def reference(queries, passages, weight, block_list, list_len):
    logit_scale = D ** -0.5
    query_emb = jnp.dot(queries, weight, preferred_element_type=jnp.float32).astype(jnp.bfloat16)
    passage_emb = jnp.dot(passages, weight, preferred_element_type=jnp.float32).astype(jnp.bfloat16)
    pass_four = passage_emb.reshape(N_DP, N_GROUP, R, D)
    query_three = query_emb.reshape(N_DP * N_GROUP, R, D)
    slot_ids = jnp.arange(N_DP, dtype=jnp.int32)

    def device_step(carry, device):
        owner = device // N_GROUP
        domain_id = device % N_GROUP
        domain = lax.dynamic_index_in_dim(pass_four, domain_id, 1, keepdims=False).reshape(N_DP * R, D)
        own_queries = lax.dynamic_index_in_dim(query_three, device, 0, keepdims=False)
        entries = lax.dynamic_index_in_dim(block_list, device, 0, keepdims=False)
        length = lax.dynamic_index_in_dim(list_len, device, 0, keepdims=False)
        listed_row = jnp.any((entries[:, None] == slot_ids[None, :]) & (slot_ids < length)[:, None], axis=0)
        loss_rows, grads = score_rows(own_queries, domain, listed_row, owner, R, logit_scale)
        query_grad = logit_scale * jnp.dot(grads, domain, preferred_element_type=jnp.float32)
        contrib = logit_scale * jnp.dot(grads.T, own_queries, preferred_element_type=jnp.float32)
        current = lax.dynamic_index_in_dim(carry, domain_id, 0, keepdims=False)
        carry = lax.dynamic_update_index_in_dim(carry, current + contrib, domain_id, 0)
        return carry, (loss_rows, query_grad)

    start = jnp.zeros((N_GROUP, N_DP * R, D), jnp.float32)
    pass_total, outputs = lax.scan(device_step, start, jnp.arange(N_DP * N_GROUP, dtype=jnp.int32))
    losses = outputs[0].reshape(TOKENS)
    query_grad = outputs[1].reshape(TOKENS, D).astype(jnp.bfloat16)
    passage_grad = pass_total.reshape(N_GROUP, N_DP, R, D).transpose(1, 0, 2, 3).reshape(TOKENS, D).astype(jnp.bfloat16)
    grad_queries = jnp.dot(query_grad, weight.T, preferred_element_type=jnp.float32).astype(jnp.bfloat16)
    grad_passages = jnp.dot(passage_grad, weight.T, preferred_element_type=jnp.float32).astype(jnp.bfloat16)
    grad_weight = jnp.dot(queries.T, query_grad, preferred_element_type=jnp.float32) + jnp.dot(passages.T, passage_grad, preferred_element_type=jnp.float32)
    return losses, grad_queries, grad_passages, grad_weight
```

```python
import math

import jax
import jax.numpy as jnp
from jax import lax
from jax.sharding import Mesh, PartitionSpec as P

SIZES = {"z": 4, "x": 4, "c": 2, "y": 4}
AXES = ("z", "x", "c", "y")
OFFSETS = (0, -1, 1, 2)
BF16 = jnp.bfloat16
F32 = jnp.float32
LAST = (((1,), (1,)), ((), ()))
FIRST = (((0,), (0,)), ((), ()))


def shift(value, axis, step):
    size = SIZES[axis]
    return lax.ppermute(value, axis, [(i, (i + step) % size) for i in range(size)])


def collect(value, axis):
    return [value] + [shift(value, axis, -step) for step in OFFSETS[1:]]


def hand_back(blocks, axis):
    return [blocks[0]] + [shift(block, axis, step) for block, step in zip(blocks[1:], OFFSETS[1:])]


def place(offset):
    return OFFSETS.index((offset + 1) % 4 - 1)


def by_offset(blocks, axis):
    me = lax.axis_index(axis)
    stacked = jnp.stack([blocks[place(o)] for o in range(4)])
    return jnp.concatenate([lax.dynamic_slice_in_dim(stacked, (i - me) % 4, 1, 0) for i in range(4)])


def dot(a, b, dims=(((1,), (0,)), ((), ()))):
    return lax.dot_general(a, b, dims, preferred_element_type=F32)


def gather_weight(weight):
    rows, width = weight.shape
    part = by_offset(collect(weight, "z"), "z")
    part = by_offset(collect(part, "x"), "x")
    part = by_offset(collect(part, "y"), "y")
    other = shift(part, "c", 1)
    core = lax.axis_index("c")
    both = jnp.stack([jnp.where(core == 0, part, other), jnp.where(core == 0, other, part)])
    return both.transpose(3, 2, 0, 1, 4, 5).reshape(-1, width)


def reduce_weight(total, rows):
    width = total.shape[1]
    parts = total.reshape(4, 4, 2, 4, rows, width).transpose(2, 3, 1, 0, 4, 5)
    core = lax.axis_index("c")
    mine = jnp.where(core == 0, parts[0], parts[1])
    theirs = jnp.where(core == 0, parts[1], parts[0])
    part = mine + shift(theirs.astype(BF16), "c", 1).astype(F32)
    for axis in ("y", "x", "z"):
        me = lax.axis_index(axis)
        pieces = [lax.dynamic_index_in_dim(part, (me + o) % 4, 0, keepdims=False) for o in OFFSETS]
        came = hand_back([pieces[0]] + [p.astype(BF16) for p in pieces[1:]], axis)
        part = sum(c.astype(F32) for c in came)
    return part


def local(queries, passages, weight, block_list, list_len):
    rows, width = queries.shape
    scale = 1.0 / math.sqrt(width)
    z, x, c, y = (lax.axis_index(a) for a in AXES)

    query_blocks = jnp.concatenate(collect(queries, "x"))
    passage_blocks = jnp.concatenate(collect(passages, "z"))
    full_weight = gather_weight(weight)

    owners = jnp.stack([(z * 4 + (x + o) % 4) * 2 + c for o in OFFSETS])
    lists = block_list[owners * 4 + y]
    lens = list_len[owners * 4 + y]
    live = jnp.arange(lists.shape[1])[None, :] < lens[:, None]

    def scored(core):
        blocks = jnp.stack([((z + o) % 4 * 4 + x) * 2 + core for o in OFFSETS])
        hit = jnp.any((lists[:, :, None] == blocks[None, None, :]) & live[:, :, None], axis=1)
        return jnp.repeat(hit, rows, axis=1)[:, None, :]

    passage_emb = dot(passage_blocks, full_weight).astype(BF16)
    other_emb = shift(passage_emb, "c", 1)
    query_emb = dot(query_blocks, full_weight).astype(BF16)

    def scores_of(emb):
        return (scale * dot(query_emb, emb, LAST)).reshape(4, rows, -1)

    scores = [scores_of(passage_emb), scores_of(other_emb)]
    masks = [scored(c), scored(1 - c)]
    own_max = jnp.maximum(*[jnp.max(jnp.where(m, s, -1e30), axis=2) for m, s in zip(masks, scores)])
    probs = [jnp.where(m, jnp.exp(s - own_max[:, :, None]), 0.0) for m, s in zip(masks, scores)]
    own_sum = sum(jnp.sum(p, axis=2) for p in probs)

    row_ids = lax.broadcasted_iota(jnp.int32, scores[0].shape, 0) * rows + lax.broadcasted_iota(
        jnp.int32, scores[0].shape, 1
    )
    col_ids = lax.broadcasted_iota(jnp.int32, scores[0].shape, 2)
    positive = (row_ids == col_ids) & (row_ids < rows)
    probs[0] = jnp.where(positive, 0.0, probs[0])
    pos_score = jnp.sum(jnp.where(positive[0], scores[0][0], 0.0), axis=1)
    probs = [p.reshape(4 * rows, -1).astype(BF16) for p in probs]

    stats = collect(jnp.stack([own_max, own_sum]), "x")
    stats = [
        jnp.stack([s[:, place(block - sender)] for block in OFFSETS], axis=1)
        for s, sender in zip(stats, OFFSETS)
    ]
    top = jnp.max(jnp.stack([s[0] for s in stats]), axis=0)
    log_total = top + jnp.log(sum(s[1] * jnp.exp(s[0] - top) for s in stats))
    factor = jnp.exp(own_max - log_total).reshape(-1, 1)
    losses = log_total[0] - pos_score
    pos_grad = (jnp.exp(pos_score - log_total[0]) - 1.0)[:, None]

    def blocks_of(value):
        return [value[i * rows : (i + 1) * rows] for i in range(4)]

    scaled_emb = (query_emb * factor).astype(BF16)
    other_part = dot(probs[1], scaled_emb, FIRST).astype(BF16)
    passage_part = dot(probs[0], scaled_emb, FIRST) + shift(other_part, "c", 1).astype(F32)
    passage_part = blocks_of(passage_part)
    passage_part[0] = passage_part[0] + pos_grad * query_emb[:rows]
    passage_low = [p.astype(BF16) for p in passage_part]
    passage_sum = sum(p.astype(F32) for p in hand_back([passage_part[0]] + passage_low[1:], "z"))

    query_part = factor * (dot(probs[0], passage_emb) + dot(probs[1], other_emb))
    query_part = blocks_of(query_part)
    query_part[0] = query_part[0] + pos_grad * passage_emb[:rows]
    query_low = [p.astype(BF16) for p in query_part]
    query_sum = sum(p.astype(F32) for p in hand_back([query_part[0]] + query_low[1:], "x"))

    weight_part = dot(query_blocks, jnp.concatenate(query_low), FIRST) + dot(
        passage_blocks, jnp.concatenate(passage_low), FIRST
    )
    grad_weight = scale * reduce_weight(weight_part, weight.shape[0])

    query_grad = (scale * query_sum).astype(BF16)
    passage_grad = (scale * passage_sum).astype(BF16)
    grad_queries = dot(query_grad, full_weight, LAST).astype(BF16)
    grad_passages = dot(passage_grad, full_weight, LAST).astype(BF16)
    return losses, grad_queries, grad_passages, grad_weight


def solution(mesh):
    grid = Mesh(mesh.devices.reshape([SIZES[a] for a in AXES]), AXES)
    table, line = P(AXES, None), P(AXES)
    return jax.shard_map(
        local,
        mesh=grid,
        in_specs=(table, table, table, P(), P()),
        out_specs=(line, table, table, table),
        check_vma=False,
    )
```

```python
import math

import jax
import jax.numpy as jnp
from jax import lax
from jax.experimental import pallas as pl
from jax.experimental.pallas import tpu as pltpu
from jax.sharding import Mesh, PartitionSpec as P

SIZES = {"z": 4, "x": 4, "c": 2, "y": 4}
AXES = ("z", "x", "c", "y")
OFFSETS = (0, -1, 1, 2)
BF16 = jnp.bfloat16
F32 = jnp.float32
LAST = (((1,), (1,)), ((), ()))
FIRST = (((0,), (0,)), ((), ()))


def swap(value):
    return lax.ppermute(value, "c", [(0, 1), (1, 0)])


def shift(value, axis, step):
    names = tuple(a for a in AXES if a in (axis, "c"))
    spots = {(i, c): 4 * c + i if axis == "y" else 2 * i + c for i in range(4) for c in range(2)}
    pairs = [(spots[i, c], spots[(i + (step, -step)[c]) % 4, c]) for i, c in spots]
    return lax.ppermute(value, names, pairs)


def collect(value, axis):
    before, after = shift(value, axis, 1), shift(value, axis, -1)
    return [value, before, after, shift(before, axis, 1)]


def place(offset):
    return OFFSETS.index((offset + 1) % 4 - 1)


def dot(a, b, dims=(((1,), (0,)), ((), ()))):
    return lax.dot_general(a, b, dims, preferred_element_type=F32)


def gather_all(weight, queries, passages):
    rows, width = weight.shape
    ring = [shift(queries, "x", 1), shift(queries, "x", -1), shift(passages, "z", 1), shift(passages, "z", -1)]
    part = lax.all_to_all(jnp.broadcast_to(weight, (16, rows, width)), ("z", "x"), 0, 0)
    part, *ring = lax.optimization_barrier((part, *ring))
    before, after = shift(part, "y", 1), shift(part, "y", -1)
    last = [shift(ring[0], "x", 1), shift(ring[2], "z", 1)]
    before, *last = lax.optimization_barrier((before, *last))
    far = shift(before, "y", 1)
    query_blocks = [queries, *ring[:2], last[0]]
    passage_blocks = [passages, *ring[2:], last[1]]
    swapped = [swap(block) for block in passage_blocks]
    far, *swapped = lax.optimization_barrier((far, *swapped))
    passage_blocks += swapped
    near = jnp.stack([part, after, before])
    near, far = (near, swap(near)), (far, swap(far))
    c, y = lax.axis_index("c"), lax.axis_index("y")
    pieces = []
    for core in range(2):
        near_one = jnp.where(c == core, near[0], near[1])
        stacked = jnp.stack([near_one[0], near_one[1], jnp.where(c == core, far[0], far[1]), near_one[2]])
        spots = [((1 - 2 * core) * (i - y)) % 4 for i in range(4)]
        pieces.append(jnp.stack([lax.dynamic_index_in_dim(stacked, spot, 0, keepdims=False) for spot in spots], axis=1))
    return jnp.stack(pieces, axis=1).reshape(-1, width), query_blocks, passage_blocks


def score_kernel(*refs):
    blocks, weight, live, raw, emb, probs, stats, own_score, scores = refs[:12], *refs[12:]
    rows, width = blocks[0].shape
    part = 4 * rows
    for i, ref in enumerate(blocks):
        raw[pl.ds(i * rows, rows), :] = ref[...]
    for i in range(3):
        for j in range(4):
            cols = pl.ds(j * width // 4, width // 4)
            emb[pl.ds(i * part, part), cols] = dot(raw[pl.ds(i * part, part), :], weight[:, cols]).astype(BF16)
    query_emb = emb[pl.ds(0, part), :]
    scale = 1.0 / math.sqrt(width)
    top = jnp.full((1, part), -1e30, F32)
    for i in range(4):
        piece = scale * dot(emb[pl.ds(part + 2 * i * rows, 2 * rows), :], query_emb, LAST)
        scores[pl.ds(2 * i * rows, 2 * rows), :] = piece
        for j in range(2):
            best = jnp.max(piece[j * rows : (j + 1) * rows], axis=0, keepdims=True)
            top = jnp.maximum(top, jnp.where(live[pl.ds(2 * i + j, 1), :] > 0.0, best, -1e30))
    total = jnp.zeros((1, part), F32)
    stats[...] = jnp.zeros_like(stats)
    own_score[...] = jnp.zeros_like(own_score)
    for i in range(8):
        base = jnp.where(live[pl.ds(i, 1), :] > 0.0, top, 1e30)
        piece = scores[pl.ds(i * rows, rows), :]
        prob = jnp.exp(piece - base)
        total = total + jnp.sum(prob, axis=0, keepdims=True)
        if i == 0:
            own = lax.broadcasted_iota(jnp.int32, prob.shape, 0) == lax.broadcasted_iota(jnp.int32, prob.shape, 1)
            prob = jnp.where(own, 0.0, prob)
            own_score[pl.ds(0, 1), :rows] = jnp.sum(jnp.where(own, piece, 0.0), axis=0, keepdims=True)[:, :rows]
        probs[pl.ds(i * rows, rows), :] = prob.astype(BF16)
    for i in range(4):
        stats[pl.ds(i, 1), :rows] = top[:, i * rows : (i + 1) * rows]
        stats[pl.ds(4 + i, 1), :rows] = total[:, i * rows : (i + 1) * rows]


def grad_kernel(
    core, here, before, after, opposite, own_score, raw, emb, probs, query_sum,
    losses, query_own, query_back, query_next, query_ahead, passage_own, passage_back, passage_next, passage_ahead,
    passage_other, mine, theirs, scaled, parts,
):
    rows, width = query_own.shape
    part = 4 * rows
    came = (here, before, after, opposite)
    columns = []
    for block in OFFSETS:
        tops = [s[pl.ds(place(block - sender), 1), :] for s, sender in zip(came, OFFSETS)]
        sums = [s[pl.ds(4 + place(block - sender), 1), :] for s, sender in zip(came, OFFSETS)]
        top = jnp.maximum(jnp.maximum(tops[0], tops[1]), jnp.maximum(tops[2], tops[3]))
        log_total = top + jnp.log(sum(s * jnp.exp(t - top) for s, t in zip(sums, tops)))
        columns.append(jnp.exp(tops[0] - log_total))
        if block == 0:
            loss = log_total - own_score[pl.ds(0, 1), :]
    columns.append(jnp.exp(-loss) - 1.0)
    losses[...] = jnp.broadcast_to(loss, losses.shape)
    columns = jnp.concatenate(columns + [jnp.zeros_like(loss)] * 3, axis=0).T
    factors = [columns[:rows, i : i + 1] for i in range(4)]
    own_factor = columns[:rows, 4:5]

    for i in range(4):
        span = pl.ds(i * rows, rows)
        scaled[span, :] = (emb[span, :].astype(F32) * factors[i]).astype(BF16)
    other = dot(probs[pl.ds(part, part), :], scaled[...]).astype(BF16)
    passage_other[...] = other
    parts[pl.ds(2 * part, part), :] = other
    for i, out in enumerate((query_own, query_back, query_next, query_ahead)):
        span = pl.ds(i * rows, rows)
        value = query_sum[span, :] * factors[i]
        if i == 0:
            value = value + own_factor * emb[pl.ds(part, rows), :].astype(F32)
        out[...] = value.astype(out.dtype)
        parts[span, :] = value.astype(BF16)
    for i, out in enumerate((passage_own, passage_back, passage_next, passage_ahead)):
        value = dot(probs[pl.ds(i * rows, rows), :], scaled[...])
        if i == 0:
            value = value + own_factor * emb[pl.ds(0, rows), :].astype(F32)
        out[...] = value.astype(out.dtype)
        parts[pl.ds(part + i * rows, rows), :] = value.astype(BF16)
    first = core[0] == 0
    for i in range(4):
        total = dot(raw[:, pl.ds(i * width // 4, width // 4)], parts[...], FIRST)
        for j in range(width // 256):
            low, high = total[64 * j : 64 * j + 32], total[64 * j + 32 : 64 * j + 64]
            span = pl.ds((i * (width // 256) + j) * 32, 32)
            mine[span, :] = jnp.where(first, low, high)
            theirs[span, :] = jnp.where(first, high, low).astype(BF16)


def local(queries, passages, weight, block_list, list_len):
    rows, width = queries.shape
    scale = 1.0 / math.sqrt(width)
    z, x, c, y = (lax.axis_index(a) for a in AXES)
    way = 1 - 2 * c

    full_weight, query_blocks, passage_blocks = gather_all(weight, queries, passages)

    owners = jnp.stack([(z * 4 + (x + way * o) % 4) * 2 + c for o in OFFSETS])
    lists = block_list[owners * 4 + y]
    lens = list_len[owners * 4 + y]
    blocks = jnp.stack(
        [((z + d * o) % 4 * 4 + x) * 2 + core for core, d in ((c, way), (1 - c, -way)) for o in OFFSETS]
    )
    live = jnp.arange(lists.shape[1])[None, :] < lens[:, None]
    hit = jnp.any((lists[None, :, :] == blocks[:, None, None]) & live[None, :, :], axis=2)
    hit = jnp.repeat(hit.astype(F32), rows, axis=1)

    shape = jax.ShapeDtypeStruct
    raw, emb, probs, stats, own_score = pl.pallas_call(
        score_kernel,
        out_shape=(
            shape((12 * rows, width), BF16),
            shape((12 * rows, width), BF16),
            shape((8 * rows, 4 * rows), BF16),
            shape((8, 256), F32),
            shape((8, 256), F32),
        ),
        scratch_shapes=[pltpu.VMEM((8 * rows, 4 * rows), F32)],
        compiler_params=pltpu.CompilerParams(vmem_limit_bytes=26 * 2**20),
        cost_estimate=pl.CostEstimate(flops=6 * 10**9, bytes_accessed=10**7, transcendentals=10**6),
        name="scores",
    )(*query_blocks, *passage_blocks, full_weight, hit)

    came = [shift(stats, "x", -o) for o in OFFSETS[1:]]
    query_sum = dot(probs, emb[4 * rows :], FIRST)
    query_sum, *came = lax.optimization_barrier((query_sum, *came))

    low, high = shape((rows, width), BF16), shape((rows, width), F32)
    losses, *query_part, own, back, following, ahead, passage_other, mine, theirs = pl.pallas_call(
        grad_kernel,
        out_shape=(
            shape((8, 256), F32),
            *(high, low, high, low) * 2,
            shape((4 * rows, width), BF16),
            shape((width // 2, width), F32),
            shape((width // 2, width), BF16),
        ),
        in_specs=[pl.BlockSpec(memory_space=pltpu.SMEM)] + [pl.BlockSpec(memory_space=pltpu.VMEM)] * 9,
        scratch_shapes=[pltpu.VMEM((4 * rows, width), BF16), pltpu.VMEM((12 * rows, width), BF16)],
        compiler_params=pltpu.CompilerParams(vmem_limit_bytes=34 * 2**20),
        cost_estimate=pl.CostEstimate(flops=6 * 10**9, bytes_accessed=10**7, transcendentals=10**4),
        name="grads",
    )(jnp.reshape(c, (1,)), stats, *came, own_score, raw, emb, probs, query_sum)

    mine = (mine + swap(theirs).astype(F32)).astype(BF16)
    weight_sum = lax.all_to_all(mine.reshape(64, -1, width), ("z", "x", "y"), 0, 0)
    grad_weight = scale * jnp.sum(weight_sum.astype(F32), axis=0)

    def finish(part, axis):
        own, back, following, ahead = part
        ahead, back = shift(ahead, axis, 1).astype(F32), shift(back, axis, -1).astype(F32)
        last = shift((following + ahead).astype(BF16), axis, 1).astype(F32)
        return dot((scale * (own + back + last)).astype(BF16), full_weight, LAST).astype(BF16)

    grad_queries = finish(query_part, "x")
    came = swap(passage_other).astype(F32)
    own, back, following, ahead = (
        (part.astype(F32) + came[i * rows : (i + 1) * rows]).astype(part.dtype)
        for i, part in enumerate((own, back, following, ahead))
    )
    grad_passages = finish((own, back, following, ahead), "z")
    return losses[0, :rows], grad_queries, grad_passages, grad_weight


def solution(mesh):
    grid = Mesh(mesh.devices.reshape([SIZES[a] for a in AXES]), AXES)
    table, line = P(AXES, None), P(AXES)
    return jax.shard_map(
        local,
        mesh=grid,
        in_specs=(table, table, table, P(), P()),
        out_specs=(line, table, table, table),
        check_vma=False,
    )
```

```python
import math

import jax
import jax.numpy as jnp
from jax import lax
from jax.experimental import pallas as pl
from jax.experimental.pallas import tpu as pltpu
from jax.sharding import Mesh, PartitionSpec as P

SIZES = {"z": 4, "x": 4, "c": 2, "y": 4}
AXES = ("z", "x", "c", "y")
WAYS = (1, -1)
OFFSETS = (0, -1, 1, 2)
BF16 = jnp.bfloat16
F32 = jnp.float32
LAST = (((1,), (1,)), ((), ()))
FIRST = (((0,), (0,)), ((), ()))


def swap(value):
    return lax.ppermute(value, "c", [(0, 1), (1, 0)])


def shift(value, axis, step):
    names = tuple(a for a in AXES if a in (axis, "c"))
    spots = {(i, c): 4 * c + i if axis == "y" else 2 * i + c for i in range(4) for c in range(2)}
    pairs = [(spots[i, c], spots[(i + step * WAYS[c]) % 4, c]) for i, c in spots]
    return lax.ppermute(value, names, pairs)


def collect(value, axis):
    before, after = shift(value, axis, 1), shift(value, axis, -1)
    return [value, before, after, shift(before, axis, 1)]


def place(offset):
    return OFFSETS.index((offset + 1) % 4 - 1)


def dot(a, b, dims=(((1,), (0,)), ((), ()))):
    return lax.dot_general(a, b, dims, preferred_element_type=F32)


def gather_all(weight, queries, passages):
    rows, width = weight.shape
    ring = [shift(queries, "x", 1), shift(queries, "x", -1), shift(passages, "z", 1), shift(passages, "z", -1)]
    part = lax.all_to_all(jnp.broadcast_to(weight, (16, rows, width)), ("z", "x"), 0, 0)
    part, *ring = lax.optimization_barrier((part, *ring))
    last = [shift(ring[0], "x", 1), shift(ring[2], "z", 1)]
    swapped = [swap(block) for block in (passages, *ring[2:])]
    part = lax.all_to_all(jnp.broadcast_to(part, (4, 16, rows, width)), "y", 0, 0)
    part, *near = lax.optimization_barrier((part, *ring, *last, *swapped))
    query_blocks = [queries, near[0], near[1], near[4]]
    passage_blocks = [passages, near[2], near[3], near[5]]
    passage_blocks += near[6:] + [swap(block) for block in passage_blocks[len(near) - 6 :]]
    other = swap(part)
    first = lax.axis_index("c") == 0
    pieces = [jnp.where(first, part, other), jnp.where(first, other, part)]
    pieces = [piece.transpose(1, 0, 2, 3) for piece in pieces]
    return jnp.stack(pieces, axis=1).reshape(-1, width), query_blocks, passage_blocks


def score_kernel(*refs):
    blocks, weight, live, raw, emb, probs, stats, own_score, scores = refs[:12], *refs[12:]
    rows, width = blocks[0].shape
    part = 4 * rows
    for i, ref in enumerate(blocks):
        raw[pl.ds(i * rows, rows), :] = ref[...]
    for i in range(3):
        for j in range(4):
            cols = pl.ds(j * width // 4, width // 4)
            emb[pl.ds(i * part, part), cols] = dot(raw[pl.ds(i * part, part), :], weight[:, cols]).astype(BF16)
    query_emb = emb[pl.ds(0, part), :]
    scale = 1.0 / math.sqrt(width)
    top = jnp.full((1, part), -1e30, F32)
    for i in range(4):
        piece = scale * dot(emb[pl.ds(part + 2 * i * rows, 2 * rows), :], query_emb, LAST)
        scores[pl.ds(2 * i * rows, 2 * rows), :] = piece
        for j in range(2):
            best = jnp.max(piece[j * rows : (j + 1) * rows], axis=0, keepdims=True)
            top = jnp.maximum(top, jnp.where(live[pl.ds(2 * i + j, 1), :] > 0.0, best, -1e30))
    total = jnp.zeros((1, part), F32)
    stats[...] = jnp.zeros_like(stats)
    own_score[...] = jnp.zeros_like(own_score)
    for i in range(8):
        base = jnp.where(live[pl.ds(i, 1), :] > 0.0, top, 1e30)
        piece = scores[pl.ds(i * rows, rows), :]
        prob = jnp.exp(piece - base)
        total = total + jnp.sum(prob, axis=0, keepdims=True)
        if i == 0:
            own = lax.broadcasted_iota(jnp.int32, prob.shape, 0) == lax.broadcasted_iota(jnp.int32, prob.shape, 1)
            prob = jnp.where(own, 0.0, prob)
            own_score[pl.ds(0, 1), :rows] = jnp.sum(jnp.where(own, piece, 0.0), axis=0, keepdims=True)[:, :rows]
        probs[pl.ds(i * rows, rows), :] = prob.astype(BF16)
    for i in range(4):
        stats[pl.ds(i, 1), :rows] = top[:, i * rows : (i + 1) * rows]
        stats[pl.ds(4 + i, 1), :rows] = total[:, i * rows : (i + 1) * rows]


def grad_kernel(
    places, here, before, after, opposite, own_score, raw, emb, probs, query_sum,
    losses, query_own, query_back, query_next, query_ahead, passage_own, passage_back, passage_next, passage_ahead,
    passage_other, mine, theirs, scaled, parts,
):
    rows, width = query_own.shape
    part, scale = 4 * rows, 1.0 / math.sqrt(width)
    came = (here, before, after, opposite)
    columns = []
    for block in OFFSETS:
        tops = [s[pl.ds(place(block - sender), 1), :] for s, sender in zip(came, OFFSETS)]
        sums = [s[pl.ds(4 + place(block - sender), 1), :] for s, sender in zip(came, OFFSETS)]
        top = jnp.maximum(jnp.maximum(tops[0], tops[1]), jnp.maximum(tops[2], tops[3]))
        log_total = top + jnp.log(sum(s * jnp.exp(t - top) for s, t in zip(sums, tops)))
        columns.append(jnp.exp(tops[0] - log_total))
        if block == 0:
            loss = log_total - own_score[pl.ds(0, 1), :]
    columns.append(jnp.exp(-loss) - 1.0)
    losses[...] = jnp.broadcast_to(loss, losses.shape)
    columns = jnp.concatenate(columns + [jnp.zeros_like(loss)] * 3, axis=0).T
    factors = [columns[:rows, i : i + 1] for i in range(4)]
    own_factor = columns[:rows, 4:5]

    for i in range(4):
        span = pl.ds(i * rows, rows)
        scaled[span, :] = (emb[span, :].astype(F32) * factors[i]).astype(BF16)
    other = dot(probs[pl.ds(part, part), :], scaled[...]).astype(BF16)
    passage_other[...] = other
    parts[pl.ds(2 * part, part), :] = other
    for i, out in enumerate((query_own, query_back, query_next, query_ahead)):
        span = pl.ds(i * rows, rows)
        value = query_sum[span, :] * factors[i]
        if i == 0:
            value = value + own_factor * emb[pl.ds(part, rows), :].astype(F32)
        out[...] = value.astype(out.dtype)
        parts[span, :] = value.astype(BF16)
    for i, out in enumerate((passage_own, passage_back, passage_next, passage_ahead)):
        value = dot(probs[pl.ds(i * rows, rows), :], scaled[...])
        if i == 0:
            value = value + own_factor * emb[pl.ds(0, rows), :].astype(F32)
        out[...] = value.astype(out.dtype)
        parts[pl.ds(part + i * rows, rows), :] = value.astype(BF16)
    first = places[0] == 0
    count = width // 256
    for i in range(4):
        total = scale * dot(raw[:, pl.ds(i * width // 4, width // 4)], parts[...], FIRST)
        for j in range(4):
            low, high = (
                jnp.concatenate([total[64 * k + 32 * c + 8 * j : 64 * k + 32 * c + 8 * j + 8] for k in range(count)])
                for c in range(2)
            )
            for out, value, spot in (
                (mine, jnp.where(first, low, high), places[1 + j]),
                (theirs, jnp.where(first, high, low), places[5 + j]),
            ):
                start = pl.multiple_of(spot * (width // 8) + i * 8 * count, 8 * count)
                out[pl.ds(start, 8 * count), :] = value.astype(BF16)


def local(queries, passages, weight, block_list, list_len):
    rows, width = queries.shape
    scale = 1.0 / math.sqrt(width)
    z, x, c, y = (lax.axis_index(a) for a in AXES)
    way, other_way = (WAYS[i] + c * (WAYS[1 - i] - WAYS[i]) for i in range(2))

    full_weight, query_blocks, passage_blocks = gather_all(weight, queries, passages)

    owners = jnp.stack([(z * 4 + (x + way * o) % 4) * 2 + c for o in OFFSETS])
    lists = block_list[owners * 4 + y]
    lens = list_len[owners * 4 + y]
    blocks = jnp.stack(
        [((z + d * o) % 4 * 4 + x) * 2 + core for core, d in ((c, way), (1 - c, other_way)) for o in OFFSETS]
    )
    live = jnp.arange(lists.shape[1])[None, :] < lens[:, None]
    hit = jnp.any((lists[None, :, :] == blocks[:, None, None]) & live[None, :, :], axis=2)
    hit = jnp.repeat(hit.astype(F32), rows, axis=1)

    shape = jax.ShapeDtypeStruct
    raw, emb, probs, stats, own_score = pl.pallas_call(
        score_kernel,
        out_shape=(
            shape((12 * rows, width), BF16),
            shape((12 * rows, width), BF16),
            shape((8 * rows, 4 * rows), BF16),
            shape((8, 256), F32),
            shape((8, 256), F32),
        ),
        scratch_shapes=[pltpu.VMEM((8 * rows, 4 * rows), F32)],
        compiler_params=pltpu.CompilerParams(vmem_limit_bytes=26 * 2**20),
        cost_estimate=pl.CostEstimate(flops=6 * 10**9, bytes_accessed=10**7, transcendentals=10**6),
        name="scores",
    )(*query_blocks, *passage_blocks, full_weight, hit)

    came = [shift(stats, "x", -o) for o in OFFSETS[1:]]
    query_sum = dot(probs, emb[4 * rows :], FIRST)
    query_sum, *came = lax.optimization_barrier((query_sum, *came))

    spots = [(d * (jnp.arange(4) - y)) % 4 for d in (way, other_way)]
    places = jnp.concatenate([c[None]] + [jnp.where(o == 0, 0, jnp.where(o == 3, 1, o + 1)) for o in spots])
    low, high = shape((rows, width), BF16), shape((rows, width), F32)
    losses, *query_part, own, back, following, ahead, passage_other, mine, theirs = pl.pallas_call(
        grad_kernel,
        out_shape=(
            shape((8, 256), F32),
            *(high, low, high, low) * 2,
            shape((4 * rows, width), BF16),
            shape((width // 2, width), BF16),
            shape((width // 2, width), BF16),
        ),
        in_specs=[pl.BlockSpec(memory_space=pltpu.SMEM)] + [pl.BlockSpec(memory_space=pltpu.VMEM)] * 9,
        scratch_shapes=[pltpu.VMEM((4 * rows, width), BF16), pltpu.VMEM((12 * rows, width), BF16)],
        compiler_params=pltpu.CompilerParams(vmem_limit_bytes=34 * 2**20),
        cost_estimate=pl.CostEstimate(flops=6 * 10**9, bytes_accessed=10**7, transcendentals=10**4),
        name="grads",
    )(places, stats, *came, own_score, raw, emb, probs, query_sum)

    def begin(part, axis):
        own, back, following, ahead = part
        return own, shift(back, axis, -1), following, shift(ahead, axis, 1)

    def go_on(part, axis):
        own, back, following, ahead = part
        last = shift((following + ahead.astype(F32)).astype(BF16), axis, 1)
        return own + back.astype(F32), last

    def finish(part, last):
        return dot((scale * (part + last.astype(F32))).astype(BF16), full_weight, LAST).astype(BF16)

    queries_part = begin(query_part, "x")
    theirs, passage_other = swap(theirs), swap(passage_other)
    weight_part = [
        (mine[i : i + width // 8].astype(F32) + theirs[i : i + width // 8].astype(F32)).astype(kind)
        for i, kind in zip(range(0, width // 2, width // 8), (F32, BF16, F32, BF16))
    ]
    weight_part[1], weight_part[3], passage_other = lax.optimization_barrier((weight_part[1], weight_part[3], passage_other))
    weight_part = begin(weight_part, "y")
    passages_part = begin(
        [
            (part.astype(F32) + passage_other[i * rows : (i + 1) * rows].astype(F32)).astype(part.dtype)
            for i, part in enumerate((own, back, following, ahead))
        ],
        "z",
    )
    weight_sum, weight_last = go_on(weight_part, "y")
    (query_sum, query_last), (passage_sum, passage_last) = go_on(queries_part, "x"), go_on(passages_part, "z")
    weight_sum = (weight_sum + weight_last.astype(F32)).astype(BF16).reshape(16, -1, width)
    grad_weight = jnp.sum(lax.all_to_all(weight_sum, ("z", "x"), 0, 0).astype(F32), axis=0)
    grad_queries, grad_passages = finish(query_sum, query_last), finish(passage_sum, passage_last)
    return losses[0, :rows], grad_queries, grad_passages, grad_weight


def solution(mesh):
    grid = Mesh(mesh.devices.reshape([SIZES[a] for a in AXES]), AXES)
    table, line = P(AXES, None), P(AXES)
    return jax.shard_map(
        local,
        mesh=grid,
        in_specs=(table, table, table, P(), P()),
        out_specs=(line, table, table, table),
        check_vma=False,
    )
```

```python
import math

import jax
import jax.numpy as jnp
from jax import lax
from jax.experimental import pallas as pl
from jax.experimental.pallas import tpu as pltpu
from jax.sharding import Mesh, PartitionSpec as P

SIZES = {"z": 4, "x": 4, "c": 2, "y": 4}
AXES = ("z", "x", "c", "y")
WAYS = (1, -1)
OFFSETS = (0, -1, 1, 2)
BF16 = jnp.bfloat16
F32 = jnp.float32
LAST = (((1,), (1,)), ((), ()))
FIRST = (((0,), (0,)), ((), ()))


def swap(value):
    return lax.ppermute(value, "c", [(0, 1), (1, 0)])


def shift(value, axis, step):
    names = tuple(a for a in AXES if a in (axis, "c"))
    spots = {(i, c): 4 * c + i if axis == "y" else 2 * i + c for i in range(4) for c in range(2)}
    pairs = [(spots[i, c], spots[(i + step * WAYS[c]) % 4, c]) for i, c in spots]
    return lax.ppermute(value, names, pairs)


def collect(value, axis):
    before, after = shift(value, axis, 1), shift(value, axis, -1)
    return [value, before, after, shift(before, axis, 1)]


def place(offset):
    return OFFSETS.index((offset + 1) % 4 - 1)


def dot(a, b, dims=(((1,), (0,)), ((), ()))):
    return lax.dot_general(a, b, dims, preferred_element_type=F32)


def gather_all(weight, queries, passages):
    rows, width = weight.shape
    ring = [shift(queries, "x", 1), shift(passages, "z", 1), shift(passages, "z", -1)]
    part = lax.all_to_all(jnp.broadcast_to(weight, (16, rows, width)), ("z", "x"), 0, 0)
    part, queries, *ring = lax.optimization_barrier((part, queries, *ring))
    ring = [ring[0], shift(queries, "x", -1), *ring[1:]]
    last = [shift(ring[0], "x", 1), shift(ring[2], "z", 1)]
    swapped = [swap(block) for block in (passages, ring[2])]
    part = lax.all_to_all(jnp.broadcast_to(part, (4, 16, rows, width)), "y", 0, 0)
    part, *near = lax.optimization_barrier((part, *ring, *last, *swapped))
    query_blocks = [queries, near[0], near[1], near[4]]
    passage_blocks = [passages, near[2], near[3], near[5]]
    passage_blocks += near[6:] + [swap(block) for block in passage_blocks[len(near) - 6 :]]
    other = swap(part)
    first = lax.axis_index("c") == 0
    pieces = [jnp.where(first, part, other), jnp.where(first, other, part)]
    pieces = [piece.transpose(1, 0, 2, 3) for piece in pieces]
    return jnp.stack(pieces, axis=1).reshape(-1, width), query_blocks, passage_blocks


def score_kernel(*refs):
    blocks, weight, live, raw, emb, probs, stats, own_score, scores = refs[:12], *refs[12:]
    rows, width = blocks[0].shape
    part = 4 * rows
    for i, ref in enumerate(blocks):
        raw[pl.ds(i * rows, rows), :] = ref[...]
    for i in range(3):
        for j in range(2):
            cols = pl.ds(j * width // 2, width // 2)
            emb[pl.ds(i * part, part), cols] = dot(raw[pl.ds(i * part, part), :], weight[:, cols]).astype(BF16)
    query_emb = emb[pl.ds(0, part), :]
    scale = 1.0 / math.sqrt(width)
    top = jnp.full((1, part), -1e30, F32)
    for i in range(2):
        piece = scale * dot(emb[pl.ds((1 + i) * part, part), :], query_emb, LAST)
        scores[pl.ds(i * part, part), :] = piece
        for j in range(4):
            best = jnp.max(piece[j * rows : (j + 1) * rows], axis=0, keepdims=True)
            top = jnp.maximum(top, jnp.where(live[pl.ds(4 * i + j, 1), :] > 0.0, best, -1e30))
    total = jnp.zeros((1, part), F32)
    stats[...] = jnp.zeros_like(stats)
    own_score[...] = jnp.zeros_like(own_score)
    for i in range(8):
        base = jnp.where(live[pl.ds(i, 1), :] > 0.0, top, 1e30)
        piece = scores[pl.ds(i * rows, rows), :]
        prob = jnp.exp(piece - base)
        total = total + jnp.sum(prob, axis=0, keepdims=True)
        if i == 0:
            own = lax.broadcasted_iota(jnp.int32, prob.shape, 0) == lax.broadcasted_iota(jnp.int32, prob.shape, 1)
            prob = jnp.where(own, 0.0, prob)
            own_score[pl.ds(0, 1), :rows] = jnp.sum(jnp.where(own, piece, 0.0), axis=0, keepdims=True)[:, :rows]
        probs[pl.ds(i * rows, rows), :] = prob.astype(BF16)
    for i in range(4):
        stats[pl.ds(i, 1), :rows] = top[:, i * rows : (i + 1) * rows]
        stats[pl.ds(4 + i, 1), :rows] = total[:, i * rows : (i + 1) * rows]


def grad_kernel(
    places, here, before, after, opposite, own_score, raw, emb, probs, query_sum,
    losses, query_own, query_back, query_next, query_ahead, passage_own, passage_back, passage_next, passage_ahead,
    passage_other, mine, theirs, scaled, parts,
):
    rows, width = query_own.shape
    part, scale = 4 * rows, 1.0 / math.sqrt(width)
    came = (here, before, after, opposite)
    columns = []
    for block in OFFSETS:
        tops = [s[pl.ds(place(block - sender), 1), :] for s, sender in zip(came, OFFSETS)]
        sums = [s[pl.ds(4 + place(block - sender), 1), :] for s, sender in zip(came, OFFSETS)]
        top = jnp.maximum(jnp.maximum(tops[0], tops[1]), jnp.maximum(tops[2], tops[3]))
        log_total = top + jnp.log(sum(s * jnp.exp(t - top) for s, t in zip(sums, tops)))
        columns.append(jnp.exp(tops[0] - log_total))
        if block == 0:
            loss = log_total - own_score[pl.ds(0, 1), :]
    columns.append(jnp.exp(-loss) - 1.0)
    losses[...] = jnp.broadcast_to(loss, losses.shape)
    columns = jnp.concatenate(columns + [jnp.zeros_like(loss)] * 3, axis=0).T
    factors = [columns[:rows, i : i + 1] for i in range(4)]
    own_factor = columns[:rows, 4:5]

    for i in range(4):
        span = pl.ds(i * rows, rows)
        scaled[span, :] = (emb[span, :].astype(F32) * factors[i]).astype(BF16)
    other = dot(probs[pl.ds(part, part), :], scaled[...]).astype(BF16)
    passage_other[...] = other
    parts[pl.ds(2 * part, part), :] = other
    for i, out in enumerate((query_own, query_back, query_next, query_ahead)):
        span = pl.ds(i * rows, rows)
        value = query_sum[span, :] * factors[i]
        if i == 0:
            value = value + own_factor * emb[pl.ds(part, rows), :].astype(F32)
        out[...] = value.astype(out.dtype)
        parts[span, :] = value.astype(BF16)
    value_all = dot(probs[pl.ds(0, part), :], scaled[...])
    for i, out in enumerate((passage_own, passage_back, passage_next, passage_ahead)):
        value = value_all[i * rows : (i + 1) * rows]
        if i == 0:
            value = value + own_factor * emb[pl.ds(0, rows), :].astype(F32)
        out[...] = value.astype(out.dtype)
        parts[pl.ds(part + i * rows, rows), :] = value.astype(BF16)
    first = places[0] == 0
    count = width // 256
    for i in range(4):
        total = scale * dot(raw[:, pl.ds(i * width // 4, width // 4)], parts[...], FIRST)
        for j in range(4):
            low, high = (
                jnp.concatenate([total[64 * k + 32 * c + 8 * j : 64 * k + 32 * c + 8 * j + 8] for k in range(count)])
                for c in range(2)
            )
            for out, value, spot in (
                (mine, jnp.where(first, low, high), places[1 + j]),
                (theirs, jnp.where(first, high, low), places[5 + j]),
            ):
                start = pl.multiple_of(spot * (width // 8) + i * 8 * count, 8 * count)
                out[pl.ds(start, 8 * count), :] = value.astype(BF16)


def local(queries, passages, weight, block_list, list_len):
    rows, width = queries.shape
    scale = 1.0 / math.sqrt(width)
    z, x, c, y = (lax.axis_index(a) for a in AXES)
    way, other_way = (WAYS[i] + c * (WAYS[1 - i] - WAYS[i]) for i in range(2))

    full_weight, query_blocks, passage_blocks = gather_all(weight, queries, passages)

    owners = jnp.stack([(z * 4 + (x + way * o) % 4) * 2 + c for o in OFFSETS])
    lists = block_list[owners * 4 + y]
    lens = list_len[owners * 4 + y]
    blocks = jnp.stack(
        [((z + d * o) % 4 * 4 + x) * 2 + core for core, d in ((c, way), (1 - c, other_way)) for o in OFFSETS]
    )
    live = jnp.arange(lists.shape[1])[None, :] < lens[:, None]
    hit = jnp.any((lists[None, :, :] == blocks[:, None, None]) & live[None, :, :], axis=2)
    hit = jnp.repeat(hit.astype(F32), rows, axis=1)

    shape = jax.ShapeDtypeStruct
    raw, emb, probs, stats, own_score = pl.pallas_call(
        score_kernel,
        out_shape=(
            shape((12 * rows, width), BF16),
            shape((12 * rows, width), BF16),
            shape((8 * rows, 4 * rows), BF16),
            shape((8, 256), F32),
            shape((8, 256), F32),
        ),
        scratch_shapes=[pltpu.VMEM((8 * rows, 4 * rows), F32)],
        compiler_params=pltpu.CompilerParams(vmem_limit_bytes=16 * 2**20),
        cost_estimate=pl.CostEstimate(flops=6 * 10**9, bytes_accessed=10**7, transcendentals=10**6),
        name="scores",
    )(*query_blocks, *passage_blocks, full_weight, hit)

    came = [shift(stats, "x", -o) for o in OFFSETS[1:]]
    query_sum = dot(probs, emb[4 * rows :], FIRST)
    query_sum, *came = lax.optimization_barrier((query_sum, *came))

    spots = [(d * (jnp.arange(4) - y)) % 4 for d in (way, other_way)]
    places = jnp.concatenate([c[None]] + [jnp.where(o == 0, 0, jnp.where(o == 3, 1, o + 1)) for o in spots])
    low, high = shape((rows, width), BF16), shape((rows, width), F32)
    losses, *query_part, own, back, following, ahead, passage_other, mine, theirs = pl.pallas_call(
        grad_kernel,
        out_shape=(
            shape((8, 256), F32),
            *(high, low, high, low) * 2,
            shape((4 * rows, width), BF16),
            shape((width // 2, width), BF16),
            shape((width // 2, width), BF16),
        ),
        in_specs=[pl.BlockSpec(memory_space=pltpu.SMEM)] + [pl.BlockSpec(memory_space=pltpu.VMEM)] * 9,
        scratch_shapes=[pltpu.VMEM((4 * rows, width), BF16), pltpu.VMEM((12 * rows, width), BF16)],
        compiler_params=pltpu.CompilerParams(vmem_limit_bytes=20 * 2**20),
        cost_estimate=pl.CostEstimate(flops=6 * 10**9, bytes_accessed=10**7, transcendentals=10**4),
        name="grads",
    )(places, stats, *came, own_score, raw, emb, probs, query_sum)

    def begin(part, axis):
        own, back, following, ahead = part
        return own, shift(back, axis, -1), following, shift(ahead, axis, 1)

    def go_on(part, axis):
        own, back, following, ahead = part
        last = shift((following + ahead.astype(F32)).astype(BF16), axis, 1)
        return own + back.astype(F32), last

    def finish(part, last):
        return dot((scale * (part + last.astype(F32))).astype(BF16), full_weight, LAST).astype(BF16)

    queries_part = begin(query_part, "x")
    theirs, passage_other = swap(theirs), swap(passage_other)
    weight_part = [
        (mine[i : i + width // 8].astype(F32) + theirs[i : i + width // 8].astype(F32)).astype(kind)
        for i, kind in zip(range(0, width // 2, width // 8), (F32, BF16, F32, BF16))
    ]
    weight_part[1], weight_part[3], passage_other = lax.optimization_barrier((weight_part[1], weight_part[3], passage_other))
    weight_part = begin(weight_part, "y")
    passages_part = begin(
        [
            (part.astype(F32) + passage_other[i * rows : (i + 1) * rows].astype(F32)).astype(part.dtype)
            for i, part in enumerate((own, back, following, ahead))
        ],
        "z",
    )
    weight_sum, weight_last = go_on(weight_part, "y")
    (query_sum, query_last), (passage_sum, passage_last) = go_on(queries_part, "x"), go_on(passages_part, "z")
    weight_sum = (weight_sum + weight_last.astype(F32)).astype(BF16).reshape(16, -1, width)
    grad_weight = jnp.sum(lax.all_to_all(weight_sum, ("z", "x"), 0, 0).astype(F32), axis=0)
    grad_queries, grad_passages = finish(query_sum, query_last), finish(passage_sum, passage_last)
    return losses[0, :rows], grad_queries, grad_passages, grad_weight


def solution(mesh):
    grid = Mesh(mesh.devices.reshape([SIZES[a] for a in AXES]), AXES)
    table, line = P(AXES, None), P(AXES)
    return jax.shard_map(
        local,
        mesh=grid,
        in_specs=(table, table, table, P(), P()),
        out_specs=(line, table, table, table),
        check_vma=False,
    )
```

```python
import math

import jax
import jax.numpy as jnp
from jax import lax
from jax.experimental import pallas as pl
from jax.experimental.pallas import tpu as pltpu
from jax.sharding import Mesh, PartitionSpec as P

SIZES = {"z": 4, "x": 4, "c": 2, "y": 4}
AXES = ("z", "x", "c", "y")
WAYS = (1, -1)
OFFSETS = (0, -1, 1, 2)
BF16 = jnp.bfloat16
F32 = jnp.float32
LAST = (((1,), (1,)), ((), ()))
FIRST = (((0,), (0,)), ((), ()))


def swap(value):
    return lax.ppermute(value, "c", [(0, 1), (1, 0)])


def shift(value, axis, step):
    names = tuple(a for a in AXES if a in (axis, "c"))
    spots = {(i, c): 4 * c + i if axis == "y" else 2 * i + c for i in range(4) for c in range(2)}
    pairs = [(spots[i, c], spots[(i + step * WAYS[c]) % 4, c]) for i, c in spots]
    return lax.ppermute(value, names, pairs)


def collect(value, axis):
    before, after = shift(value, axis, 1), shift(value, axis, -1)
    return [value, before, after, shift(before, axis, 1)]


def place(offset):
    return OFFSETS.index((offset + 1) % 4 - 1)


def dot(a, b, dims=(((1,), (0,)), ((), ()))):
    return lax.dot_general(a, b, dims, preferred_element_type=F32)


def gather_all(weight, queries, passages):
    rows, width = weight.shape
    ring = [shift(queries, "x", 1), shift(passages, "z", 1), shift(passages, "z", -1)]
    part = lax.all_to_all(jnp.broadcast_to(weight, (16, rows, width)), ("z", "x"), 0, 0)
    part, queries, *ring = lax.optimization_barrier((part, queries, *ring))
    ring = [ring[0], shift(queries, "x", -1), *ring[1:]]
    last = [shift(ring[0], "x", 1), shift(ring[2], "z", 1)]
    swapped = [swap(block) for block in (passages, ring[2])]
    part = lax.all_to_all(jnp.broadcast_to(part, (4, 16, rows, width)), "y", 0, 0)
    part, *near = lax.optimization_barrier((part, *ring, *last, *swapped))
    query_blocks = [queries, near[0], near[1], near[4]]
    passage_blocks = [passages, near[2], near[3], near[5]]
    passage_blocks += near[6:] + [swap(block) for block in passage_blocks[len(near) - 6 :]]
    other = swap(part)
    first = lax.axis_index("c") == 0
    pieces = [jnp.where(first, part, other), jnp.where(first, other, part)]
    pieces = [piece.transpose(1, 0, 2, 3) for piece in pieces]
    return jnp.stack(pieces, axis=1).reshape(-1, width), query_blocks, passage_blocks


def score_kernel(*refs):
    blocks, weight, live, raw, emb, probs, stats, own_score, scores = refs[:12], *refs[12:]
    rows, width = blocks[0].shape
    part = 4 * rows
    for i, ref in enumerate(blocks):
        raw[pl.ds(i * rows, rows), :] = ref[...]
    for i in range(3):
        for j in range(2):
            cols = pl.ds(j * width // 2, width // 2)
            emb[pl.ds(i * part, part), cols] = dot(raw[pl.ds(i * part, part), :], weight[:, cols]).astype(BF16)
    query_emb = emb[pl.ds(0, part), :]
    scale = 1.0 / math.sqrt(width)
    top = jnp.full((1, part), -1e30, F32)
    for i in range(2):
        piece = scale * dot(emb[pl.ds((1 + i) * part, part), :], query_emb, LAST)
        scores[pl.ds(i * part, part), :] = piece
        for j in range(4):
            best = jnp.max(piece[j * rows : (j + 1) * rows], axis=0, keepdims=True)
            top = jnp.maximum(top, jnp.where(live[pl.ds(4 * i + j, 1), :] > 0.0, best, -1e30))
    total = jnp.zeros((1, part), F32)
    stats[...] = jnp.zeros_like(stats)
    own_score[...] = jnp.zeros_like(own_score)
    for i in range(8):
        base = jnp.where(live[pl.ds(i, 1), :] > 0.0, top, 1e30)
        piece = scores[pl.ds(i * rows, rows), :]
        prob = jnp.exp(piece - base)
        total = total + jnp.sum(prob, axis=0, keepdims=True)
        if i == 0:
            own = lax.broadcasted_iota(jnp.int32, prob.shape, 0) == lax.broadcasted_iota(jnp.int32, prob.shape, 1)
            prob = jnp.where(own, 0.0, prob)
            own_score[pl.ds(0, 1), :rows] = jnp.sum(jnp.where(own, piece, 0.0), axis=0, keepdims=True)[:, :rows]
        probs[pl.ds(i * rows, rows), :] = prob.astype(BF16)
    for i in range(4):
        stats[pl.ds(i, 1), :rows] = top[:, i * rows : (i + 1) * rows]
        stats[pl.ds(4 + i, 1), :rows] = total[:, i * rows : (i + 1) * rows]


def grad_kernel(
    places, here, before, after, opposite, own_score, raw, emb, probs, query_sum,
    losses, query_own, query_back, query_next, query_ahead, passage_own, passage_back, passage_next, passage_ahead,
    passage_other, mine, theirs, scaled, parts,
):
    rows, width = query_own.shape
    part, scale = 4 * rows, 1.0 / math.sqrt(width)
    came = (here, before, after, opposite)
    columns = []
    for block in OFFSETS:
        tops = [s[pl.ds(place(block - sender), 1), :] for s, sender in zip(came, OFFSETS)]
        sums = [s[pl.ds(4 + place(block - sender), 1), :] for s, sender in zip(came, OFFSETS)]
        top = jnp.maximum(jnp.maximum(tops[0], tops[1]), jnp.maximum(tops[2], tops[3]))
        log_total = top + jnp.log(sum(s * jnp.exp(t - top) for s, t in zip(sums, tops)))
        columns.append(jnp.exp(tops[0] - log_total))
        if block == 0:
            loss = log_total - own_score[pl.ds(0, 1), :]
    columns.append(jnp.exp(-loss) - 1.0)
    losses[...] = jnp.broadcast_to(loss, losses.shape)
    columns = jnp.concatenate(columns + [jnp.zeros_like(loss)] * 3, axis=0).T
    factors = [columns[:rows, i : i + 1] for i in range(4)]
    own_factor = columns[:rows, 4:5]

    for i in range(4):
        span = pl.ds(i * rows, rows)
        scaled[span, :] = (emb[span, :].astype(F32) * factors[i]).astype(BF16)
    other = dot(probs[pl.ds(part, part), :], scaled[...]).astype(BF16)
    passage_other[...] = other
    parts[pl.ds(2 * part, part), :] = other
    for i, out in enumerate((query_own, query_back, query_next, query_ahead)):
        span = pl.ds(i * rows, rows)
        value = query_sum[span, :] * factors[i]
        if i == 0:
            value = value + own_factor * emb[pl.ds(part, rows), :].astype(F32)
        out[...] = value.astype(out.dtype)
        parts[span, :] = value.astype(BF16)
    value_all = dot(probs[pl.ds(0, part), :], scaled[...])
    for i, out in enumerate((passage_own, passage_back, passage_next, passage_ahead)):
        value = value_all[i * rows : (i + 1) * rows]
        if i == 0:
            value = value + own_factor * emb[pl.ds(0, rows), :].astype(F32)
        out[...] = value.astype(out.dtype)
        parts[pl.ds(part + i * rows, rows), :] = value.astype(BF16)
    first = places[0] == 0
    count = width // 256
    for i in range(4):
        total = scale * dot(raw[:, pl.ds(i * width // 4, width // 4)], parts[...], FIRST)
        for j in range(4):
            low, high = (
                jnp.concatenate([total[64 * k + 32 * c + 8 * j : 64 * k + 32 * c + 8 * j + 8] for k in range(count)])
                for c in range(2)
            )
            for out, value, spot in (
                (mine, jnp.where(first, low, high), places[1 + j]),
                (theirs, jnp.where(first, high, low), places[5 + j]),
            ):
                start = pl.multiple_of(spot * (width // 8) + i * 8 * count, 8 * count)
                out[pl.ds(start, 8 * count), :] = value.astype(BF16)


def local(queries, passages, weight, block_list, list_len):
    rows, width = queries.shape
    scale = 1.0 / math.sqrt(width)
    z, x, c, y = (lax.axis_index(a) for a in AXES)
    way, other_way = (WAYS[i] + c * (WAYS[1 - i] - WAYS[i]) for i in range(2))

    full_weight, query_blocks, passage_blocks = gather_all(weight, queries, passages)

    owners = jnp.stack([(z * 4 + (x + way * o) % 4) * 2 + c for o in OFFSETS])
    lists = block_list[owners * 4 + y]
    lens = list_len[owners * 4 + y]
    blocks = jnp.stack(
        [((z + d * o) % 4 * 4 + x) * 2 + core for core, d in ((c, way), (1 - c, other_way)) for o in OFFSETS]
    )
    live = jnp.arange(lists.shape[1])[None, :] < lens[:, None]
    hit = jnp.any((lists[None, :, :] == blocks[:, None, None]) & live[None, :, :], axis=2)
    hit = jnp.repeat(hit.astype(F32), rows, axis=1)

    shape = jax.ShapeDtypeStruct
    raw, emb, probs, stats, own_score = pl.pallas_call(
        score_kernel,
        out_shape=(
            shape((12 * rows, width), BF16),
            shape((12 * rows, width), BF16),
            shape((8 * rows, 4 * rows), BF16),
            shape((8, 256), F32),
            shape((8, 256), F32),
        ),
        scratch_shapes=[pltpu.VMEM((8 * rows, 4 * rows), F32)],
        compiler_params=pltpu.CompilerParams(vmem_limit_bytes=16 * 2**20),
        cost_estimate=pl.CostEstimate(flops=6 * 10**9, bytes_accessed=10**7, transcendentals=10**6),
        name="scores",
    )(*query_blocks, *passage_blocks, full_weight, hit)

    came = [shift(stats, "x", -o) for o in OFFSETS[1:]]
    query_sum = dot(probs, emb[4 * rows :], FIRST)
    query_sum, *came = lax.optimization_barrier((query_sum, *came))

    spots = [(d * (jnp.arange(4) - y)) % 4 for d in (way, other_way)]
    places = jnp.concatenate([c[None]] + [jnp.where(o == 0, 0, jnp.where(o == 3, 1, o + 1)) for o in spots])
    low, high = shape((rows, width), BF16), shape((rows, width), F32)
    losses, *query_part, own, back, following, ahead, passage_other, mine, theirs = pl.pallas_call(
        grad_kernel,
        out_shape=(
            shape((8, 256), F32),
            *(high, low, high, low) * 2,
            shape((4 * rows, width), BF16),
            shape((width // 2, width), BF16),
            shape((width // 2, width), BF16),
        ),
        in_specs=[pl.BlockSpec(memory_space=pltpu.SMEM)] + [pl.BlockSpec(memory_space=pltpu.VMEM)] * 9,
        scratch_shapes=[pltpu.VMEM((4 * rows, width), BF16), pltpu.VMEM((12 * rows, width), BF16)],
        compiler_params=pltpu.CompilerParams(vmem_limit_bytes=20 * 2**20),
        cost_estimate=pl.CostEstimate(flops=6 * 10**9, bytes_accessed=10**7, transcendentals=10**4),
        name="grads",
    )(places, stats, *came, own_score, raw, emb, probs, query_sum)

    def begin(part, axis):
        own, back, following, ahead = part
        return own, shift(back, axis, -1), following, shift(ahead, axis, 1)

    def go_on(part, axis):
        own, back, following, ahead = part
        last = shift((following + ahead.astype(F32)).astype(BF16), axis, 1)
        return own + back.astype(F32), last

    def finish(part, last):
        return dot((scale * (part + last.astype(F32))).astype(BF16), full_weight, LAST).astype(BF16)

    queries_part = (*query_part[:3], shift(query_part[3], "x", 1))
    theirs, passage_other = swap(theirs), swap(passage_other)
    weight_part = [
        (mine[i : i + width // 8].astype(F32) + theirs[i : i + width // 8].astype(F32)).astype(kind)
        for i, kind in zip(range(0, width // 2, width // 8), (F32, BF16, F32, BF16))
    ]
    weight_part[1], weight_part[3], passage_other = lax.optimization_barrier((weight_part[1], weight_part[3], passage_other))
    weight_part = begin(weight_part, "y")
    passages_part = begin(
        [
            (part.astype(F32) + passage_other[i * rows : (i + 1) * rows].astype(F32)).astype(part.dtype)
            for i, part in enumerate((own, back, following, ahead))
        ],
        "z",
    )
    ahead, back = lax.optimization_barrier((weight_part[3], queries_part[1]))
    weight_part = (*weight_part[:3], ahead)
    queries_part = (queries_part[0], shift(back, "x", -1), *queries_part[2:])
    weight_sum, weight_last = go_on(weight_part, "y")
    (query_sum, query_last), (passage_sum, passage_last) = go_on(queries_part, "x"), go_on(passages_part, "z")
    weight_sum = (weight_sum + weight_last.astype(F32)).astype(BF16).reshape(16, -1, width)
    grad_weight = jnp.sum(lax.all_to_all(weight_sum, ("z", "x"), 0, 0).astype(F32), axis=0)
    grad_queries, grad_passages = finish(query_sum, query_last), finish(passage_sum, passage_last)
    return losses[0, :rows], grad_queries, grad_passages, grad_weight


def solution(mesh):
    grid = Mesh(mesh.devices.reshape([SIZES[a] for a in AXES]), AXES)
    table, line = P(AXES, None), P(AXES)
    return jax.shard_map(
        local,
        mesh=grid,
        in_specs=(table, table, table, P(), P()),
        out_specs=(line, table, table, table),
        check_vma=False,
    )
```
